256 devices in a mesh: phase: 2 (over core), tok: 32 (over z, x), mp: 4 (over y).
Axes of the slice: x: 4, y: 4, z: 8, core: 2. Of those that a mesh axis runs over, the one named last changes fastest.
Arguments:
- hidden: bfloat16 [2, 4096, 6656], P('phase', 'tok', 'mp'), may hold values from -30 to 30
- w_qkv: bfloat16 [2, 6656, 3, 4096], P('phase', 'mp', None, 'tok'), may hold values from -1 to 1
- segment_ids: int32 [2, 4096], P('phase'), may hold values from 0 to 3, never falling along the last dimension, each value on 1 to 2048 neighbouring positions
- exit_flags: int32 [2, 32], P('phase'), may hold values from 0 to 1, as said below
Outputs:
- attended: bfloat16 [2, 4096, 4096], P('phase', 'mp', 'tok')
- handed: bfloat16 [2, 4096, 4096], P('phase', 'mp', 'tok')
The draws below stay inside these ranges and needn't reach their ends.
Inputs may be any that keep to these rules, and one draw needn't show every extreme that they name: `exit_flags`: in each micro-batch exactly 16 of the 32 blocks have flag 0.
All inputs are finite; a program needn't handle non-finite values.
Results may differ from the reference program's by a relative error of at most 0.0068.
Values may be sent and summed in bfloat16 or wider, within the bound.
No kernel may reach another device: no remote copies, remote signals or barrier semaphores. Data moves between devices by JAX's collectives and lax.ppermute only.
A program may use at most 64 MiB of HBM per device.

```python
import math
import jax
import jax.numpy as jnp
import numpy as np
from jax import lax

D = 6656
HEADS = 32
HEAD = 128
BLOCK = 128
SEGS = 4
TOKENS = 4096
BLOCKS = 32
SURV_BLK = 16
N_PHASE = 2


def draw_hidden(key, part):
    first = jax.random.fold_in(key, 11)
    rows = jnp.clip(jax.random.normal(first, (N_PHASE, TOKENS, D), jnp.float32), -6.0, 6.0)
    return rows.astype(jnp.bfloat16)


def draw_w_qkv(key, part):
    first = jax.random.fold_in(key, 21)
    weights = jnp.clip(jax.random.normal(first, (N_PHASE, D, 3, HEADS * HEAD), jnp.float32), -4.0, 4.0) / math.sqrt(D)
    return weights.astype(jnp.bfloat16)


def draw_exit_flags(key, part):
    first = jax.random.fold_in(key, 31)
    phase_keys = jax.random.split(first, N_PHASE)
    ranks = jax.vmap(lambda one: jax.random.permutation(one, BLOCKS))(phase_keys)
    return (ranks >= SURV_BLK).astype(jnp.int32)


def length_profile(count, total, bound, lean):
    portions = [(1 << 20) // math.isqrt(grade ** lean) + 1 for grade in range(2, count + 1)]
    rest, counts = total - bound - (count - 1), [1] * (count - 1)
    while rest > 0:
        candidates = [i for i in range(count - 1) if counts[i] < bound]
        mass, remaining = sum([portions[i] for i in candidates]), rest
        for i in candidates:
            more = min(bound - counts[i], max(1, remaining * portions[i] // mass), rest)
            counts[i] = counts[i] + more
            rest = rest - more
    return np.array([bound] + counts)


def ragged_sizes(key, number_of, total, most, skew):
    if number_of == 2:
        one = jax.random.randint(key, (), max(1, total - most), min(most, total - 1) + 1)
        return jnp.stack([one, total - one])
    tallies = jnp.asarray(length_profile(number_of, total, most, skew), jnp.int32)
    pairs = (number_of - 1) // 2
    giver, taker = tallies[1:1 + 2 * pairs:2], tallies[2:2 + 2 * pairs:2]
    slack = jnp.minimum(giver - 1, most - taker)
    passed = jax.random.randint(jax.random.fold_in(key, 1), (pairs,), 0, 1 << 20) % (slack + 1)
    tallies = tallies.at[1:1 + 2 * pairs:2].set(giver - passed).at[2:2 + 2 * pairs:2].set(taker + passed)
    return tallies[jax.random.permutation(jax.random.fold_in(key, 2), number_of)]


def setup_inputs(seed: int = 0) -> dict:
    key_of = jax.random.split(jax.random.key(seed), 5)
    hidden = draw_hidden(jax.random.fold_in(key_of[4], 71), 0)
    w_qkv = draw_w_qkv(jax.random.fold_in(key_of[4], 71), 0)
    segment_ids = jax.vmap(lambda own: jnp.searchsorted(jnp.cumsum(ragged_sizes(own, SEGS, TOKENS, TOKENS // 2, 0)), jnp.arange(TOKENS), side="right"))(jax.random.split(key_of[2], N_PHASE)).reshape((N_PHASE, TOKENS)).astype(jnp.int32)
    exit_flags = draw_exit_flags(jax.random.fold_in(key_of[4], 71), 0)
    return dict(hidden=hidden, w_qkv=w_qkv, segment_ids=segment_ids, exit_flags=exit_flags)


def attend_head(trio, segment):
    query, keys, values = trio
    total = query.shape[0]
    scores = jnp.dot(query, keys.T, preferred_element_type=jnp.float32) * (1.0 / math.sqrt(HEAD))
    positions = jnp.arange(total, dtype=jnp.int32)
    allowed = (positions[None, :] <= positions[:, None]) & (segment[None, :] == segment[:, None])
    scores = jnp.where(allowed, scores, -1e+30)
    peak = lax.optimization_barrier(jnp.max(scores, axis=-1, keepdims=True))
    expo = jnp.exp(scores - peak)
    probs = (expo / lax.optimization_barrier(jnp.sum(expo, axis=-1, keepdims=True))).astype(jnp.bfloat16)
    return jnp.dot(probs, values, preferred_element_type=jnp.float32)

def reference(hidden, w_qkv, segment_ids, exit_flags):
    results = []
    for phase in range(N_PHASE):
        rows = hidden[phase]
        query = jnp.dot(rows, w_qkv[phase, :, 0, :], preferred_element_type=jnp.float32).astype(jnp.bfloat16)
        keys = jnp.dot(rows, w_qkv[phase, :, 1, :], preferred_element_type=jnp.float32).astype(jnp.bfloat16)
        values = jnp.dot(rows, w_qkv[phase, :, 2, :], preferred_element_type=jnp.float32).astype(jnp.bfloat16)

        def split_heads(matrix):
            return matrix.reshape(TOKENS, HEADS, HEAD).transpose(1, 0, 2)
        segment = segment_ids[phase]
        mixed = lax.map(lambda trio: attend_head(trio, segment), (split_heads(query), split_heads(keys), split_heads(values)))
        mixed = mixed.transpose(1, 0, 2).reshape(TOKENS, HEADS * HEAD)
        alive = jnp.repeat(exit_flags[phase] == 0, BLOCK)
        results.append(jnp.where(alive[:, None], mixed, 0.0).astype(jnp.bfloat16))
    attended = jnp.stack(results)
    handed = jnp.roll(attended, 1, axis=0)
    return (attended, handed)
```

```python
import functools
import math

import jax
import jax.numpy as jnp
from jax import lax
from jax.experimental import pallas as pl
from jax.experimental.pallas import tpu as pltpu
from jax.sharding import Mesh
from jax.sharding import PartitionSpec as P

HEAD = 128
BLOCK = 128
CHUNK = 512
VMEM = pl.BlockSpec(memory_space=pltpu.VMEM)
SMEM = pl.BlockSpec(memory_space=pltpu.SMEM)


def send(block, axis, distance):
    n = lax.axis_size(axis)
    return lax.ppermute(block, axis, [(i, (i + distance) % n) for i in range(n)])


def gather_ring4(part):
    half = part.shape[0] // 2
    left = send(part, "x", 1)
    right = send(part, "x", -1)
    top = send(right[:half], "x", -1)
    bottom = send(left[half:], "x", 1)
    return part, right, top, bottom, left


def project_kernel(shift_ref, rows_ref, own, right, top, bottom, left, out0, out1, out2, out3, cat):
    half = top.shape[0]

    @pl.when(pl.program_id(0) == 0)
    def _():
        for k in range(4):
            slot = lax.rem(k + 4 - shift_ref[0], 4)
            columns = slice(k * HEAD, (k + 1) * HEAD)

            @pl.when(slot == 0)
            def _():
                cat[:, columns] = own[...]

            @pl.when(slot == 1)
            def _():
                cat[:, columns] = right[...]

            @pl.when(slot == 2)
            def _():
                cat[:half, columns] = top[...]
                cat[half:, columns] = bottom[...]

            @pl.when(slot == 3)
            def _():
                cat[:, columns] = left[...]

    product = jnp.dot(rows_ref[...], cat[...], preferred_element_type=jnp.float32)
    out0[...] = product[:, :HEAD]
    for k, out in enumerate((out1, out2, out3), 1):
        out[...] = product[:, k * HEAD : (k + 1) * HEAD].astype(jnp.bfloat16)


def project(shift, rows, weights):
    total, width = rows.shape
    step = 256
    whole = lambda i: (0, 0)
    out = pl.BlockSpec((step, HEAD), lambda i: (i, 0))
    return pl.pallas_call(
        project_kernel,
        grid=(total // step,),
        in_specs=[SMEM, pl.BlockSpec((step, width), lambda i: (i, 0))]
        + [pl.BlockSpec(w.shape, whole) for w in weights],
        out_specs=[out] * 4,
        out_shape=[jax.ShapeDtypeStruct((total, HEAD), jnp.float32)]
        + [jax.ShapeDtypeStruct((total, HEAD), jnp.bfloat16)] * 3,
        scratch_shapes=[pltpu.VMEM((width, 4 * HEAD), jnp.bfloat16)],
        cost_estimate=pl.CostEstimate(
            flops=2 * total * width * 4 * HEAD, bytes_accessed=7 * 2**20, transcendentals=0
        ),
        compiler_params=pltpu.CompilerParams(vmem_limit_bytes=32 * 2**20),
    )(shift, rows, *weights)


def sum_over_y(parts):
    own, one, two, three = parts
    total = own
    for k, part in ((1, one), (3, three), (2, two)):
        total = total + send(part, "y", k).astype(jnp.float32)
    return total.astype(jnp.bfloat16)


def gather_x(block):
    return block, send(block, "x", -1), send(block, "x", -2), send(block, "x", -3)


def attend_kernel(scal_ref, flag_ref, q_ref, *refs):
    ks, vs, outs = refs[:4], refs[4:8], refs[8:12]
    kfull, vfull, scores = refs[12:]
    x = scal_ref[0]
    c1, c2, c3 = scal_ref[1], scal_ref[2], scal_ref[3]
    blocks = q_ref.shape[0] // BLOCK
    for r in range(4):
        lane = lax.rem(x + r, 4)
        for z in range(blocks):
            at = pl.ds(pl.multiple_of((4 * z + lane) * BLOCK, BLOCK), BLOCK)
            kfull[at, :] = ks[r][z * BLOCK : (z + 1) * BLOCK, :]
            vfull[at, :] = vs[r][z * BLOCK : (z + 1) * BLOCK, :]

    def first(i):
        return jnp.where(i >= c3, c3, jnp.where(i >= c2, c2, jnp.where(i >= c1, c1, 0)))

    for s in range(4):
        for t in range(2):
            z = 2 * lax.rem(x + s, 4) + t
            block = 4 * z + x
            out = outs[s]
            mine = slice(t * BLOCK, (t + 1) * BLOCK)

            @pl.when(flag_ref[block] != 0)
            def _():
                out[mine, :] = jnp.zeros((BLOCK, HEAD), jnp.bfloat16)

            @pl.when(flag_ref[block] == 0)
            def _():
                base = block * BLOCK
                low = lax.div(first(base), CHUNK)
                high = lax.div(base, CHUNK) + 1
                query = q_ref[pl.ds(pl.multiple_of(z * BLOCK, BLOCK), BLOCK), :]
                row = base + lax.broadcasted_iota(jnp.int32, (BLOCK, CHUNK), 0)
                column = lax.broadcasted_iota(jnp.int32, (BLOCK, CHUNK), 1)
                begin = first(row)

                def score(c, peak):
                    at = pl.multiple_of(c * CHUNK, CHUNK)
                    value = lax.dot_general(
                        query,
                        kfull[pl.ds(at, CHUNK), :],
                        (((1,), (1,)), ((), ())),
                        preferred_element_type=jnp.float32,
                    ) * (1.0 / math.sqrt(HEAD))
                    place = column + at
                    value = jnp.where((place <= row) & (place >= begin), value, -1e30)
                    scores[c - low] = value
                    return jnp.maximum(peak, jnp.max(value, axis=-1, keepdims=True))

                peak = lax.fori_loop(
                    low, high, score, jnp.full((BLOCK, 1), -1e30, jnp.float32)
                )

                def mix(c, carry):
                    norm, mixed = carry
                    at = pl.multiple_of(c * CHUNK, CHUNK)
                    expo = jnp.exp(scores[c - low] - peak)
                    norm = norm + jnp.sum(expo, axis=-1, keepdims=True)
                    mixed = mixed + jnp.dot(
                        expo.astype(jnp.bfloat16),
                        vfull[pl.ds(at, CHUNK), :],
                        preferred_element_type=jnp.float32,
                    )
                    return norm, mixed

                norm, mixed = lax.fori_loop(
                    low,
                    high,
                    mix,
                    (jnp.zeros((BLOCK, 1), jnp.float32), jnp.zeros((BLOCK, HEAD), jnp.float32)),
                )
                out[mine, :] = (mixed / norm).astype(jnp.bfloat16)


def attend(scalars, flags, query, keys, values):
    rows = query.shape[0]
    tokens = 4 * rows
    quarter = jax.ShapeDtypeStruct((rows // 4, HEAD), jnp.bfloat16)
    return pl.pallas_call(
        attend_kernel,
        in_specs=[SMEM, SMEM] + [VMEM] * 9,
        out_specs=[VMEM] * 4,
        out_shape=[quarter] * 4,
        scratch_shapes=[
            pltpu.VMEM((tokens, HEAD), jnp.bfloat16),
            pltpu.VMEM((tokens, HEAD), jnp.bfloat16),
            pltpu.VMEM((tokens // CHUNK, BLOCK, CHUNK), jnp.float32),
        ],
        cost_estimate=pl.CostEstimate(
            flops=2 * rows * 2048 * HEAD, bytes_accessed=3 * 2**20, transcendentals=rows * 1024
        ),
        compiler_params=pltpu.CompilerParams(vmem_limit_bytes=32 * 2**20),
    )(scalars, flags, query, *keys, *values)


def place_kernel(y_ref, *refs):
    parts, out = refs[:4], refs[4]
    for s in range(4):
        x = lax.rem(y_ref[0] + 4 - s, 4)
        for t in range(2):
            at = pl.ds(pl.multiple_of((4 * t + x) * BLOCK, BLOCK), BLOCK)
            out[at, :] = parts[s][t * BLOCK : (t + 1) * BLOCK, :]


def place(y, parts):
    rows = 4 * parts[0].shape[0]
    return pl.pallas_call(
        place_kernel,
        in_specs=[SMEM] + [VMEM] * 4,
        out_specs=VMEM,
        out_shape=jax.ShapeDtypeStruct((rows, HEAD), jnp.bfloat16),
    )(y, *parts)


def local(hidden, w_qkv, segment_ids, exit_flags):
    x, y = lax.axis_index("x"), lax.axis_index("y")
    weights = w_qkv[0]
    segment = segment_ids[0]
    bounds = [jnp.sum((segment < s).astype(jnp.int32)) for s in (1, 2, 3)]
    scalars = jnp.stack([x.astype(jnp.int32)] + bounds)
    shift = lax.rem(x - y + 4, 4).astype(jnp.int32).reshape(1)
    rows = lax.all_gather(hidden[0], "z", axis=0, tiled=True)
    sums = [
        sum_over_y(project(shift, rows, gather_ring4(weights[:, part, :]))) for part in (1, 2, 0)
    ]
    keys, values, query = sums
    mixed = attend(scalars, exit_flags[0], query, gather_x(keys), gather_x(values))
    moved = [
        lax.ppermute(
            mixed[s],
            ("x", "y"),
            [(4 * i + j, 4 * j + (i + s) % 4) for i in range(4) for j in range(4)],
        )
        for s in range(4)
    ]
    result = place(y.astype(jnp.int32).reshape(1), moved)
    handed = send(result, "phase", 1)
    return (result[None], handed[None])


def solution(mesh):
    split = Mesh(mesh.devices.reshape(2, 8, 4, 4), ("phase", "z", "x", "y"))
    tok = ("z", "x")
    in_specs = (
        P("phase", tok, "y"),
        P("phase", "y", None, tok),
        P("phase", None),
        P("phase", None),
    )
    out_specs = (P("phase", "y", tok), P("phase", "y", tok))
    return jax.shard_map(local, mesh=split, in_specs=in_specs, out_specs=out_specs, check_vma=False)
```

```python
import functools
import math

import jax
import jax.numpy as jnp
from jax import lax
from jax.experimental import pallas as pl
from jax.experimental.pallas import tpu as pltpu
from jax.sharding import Mesh
from jax.sharding import PartitionSpec as P

HEAD = 128
BLOCK = 128
SPAN = 256
LONGEST = 9
EARLY = (0, 1, 2, 6, 7)
LATE = (3, 4, 5)
CUT = 896
BRIEF = pl.CostEstimate(flops=1, bytes_accessed=1, transcendentals=0)
LONG = pl.CostEstimate(flops=3 * 10**10, bytes_accessed=1, transcendentals=0)
VMEM = pl.BlockSpec(memory_space=pltpu.VMEM)
FAR = pl.BlockSpec(memory_space=pltpu.HBM)
SMEM = pl.BlockSpec(memory_space=pltpu.SMEM)
LIMIT = pltpu.CompilerParams(vmem_limit_bytes=32 * 2**20)


def send(block, axis, distance):
    n = lax.axis_size(axis)
    return lax.ppermute(block, axis, [(i, (i + distance) % n) for i in range(n)])


def after(values, *earlier):
    return lax.optimization_barrier((values, earlier))[0]


def gather_x_ring(part, earlier, second):
    left = send(part, "x", 1)
    right = send(part, "x", -1)
    top = send(after(right, earlier)[:CUT], "x", -1)
    bottom = send(after(left, second)[CUT:], "x", 1)
    return {0: (part,), 1: (right,), 3: (left,), 2: (top, bottom)}


def gather_x_by_right(block, *earlier):
    right = send(block, "x", -1)
    return block, right, send(after(right, earlier), "x", -1), send(block, "x", 1)


def gather_z_ring(block):
    found = {0: [block]}
    left = right = block
    for step in (1, 2, 3):
        left, right = send(left, "z", 1), send(right, "z", -1)
        found[8 - step], found[step] = [left], [right]
    found[4] = [send(left, "z", 1)]
    return found


def fill_rows(pieces, rows):
    at = 0
    for piece in pieces:
        rows[at : at + piece.shape[0], :] = piece[...]
        at += piece.shape[0]


def product_of(rows, weights):
    total, at = None, 0
    for weight in weights:
        width = weight.shape[0]
        term = jnp.dot(
            rows[:, at : at + width], weight[...], preferred_element_type=jnp.float32
        )
        total = term if total is None else total + term
        at += width
    return total


def cut_by(counts, refs):
    groups, at = [], 0
    for count in counts:
        groups.append(refs[at : at + count])
        at += count
    return groups


def store_for(outs, shift, slot, product):
    target = lax.rem(slot + shift, 4)
    if len(outs) == 1:
        outs[0][target] = product.astype(outs[0].dtype)
        return
    for k in range(4):

        @pl.when(target == k)
        def _():
            outs[k][...] = product.astype(outs[k].dtype)


def project_kernel(shift_ref, *refs, pieces, slots, counts):
    total = sum(counts)
    weights = cut_by(counts, refs[pieces : pieces + total])
    outs = refs[pieces + total : -1]
    rows = refs[-1]
    fill_rows(refs[:pieces], rows)
    if len(outs) == 2:
        outs[1][...] = jnp.zeros_like(outs[1])
        outs = outs[:1]
    for slot, weight in zip(slots, weights):
        store_for(outs, shift_ref[0], slot, product_of(rows, weight))


def project_rest_kernel(x_ref, *refs, pieces, slot):
    weights = refs[pieces : pieces + 2]
    out = refs[pieces + 3]
    rows, result, sem = refs[pieces + 4 :]
    fill_rows(refs[:pieces], rows)
    result[...] = product_of(rows, weights).astype(result.dtype)
    copy = pltpu.make_async_copy(result, out.at[lax.rem(slot + x_ref[0], 4)], sem)
    copy.start()
    copy.wait()


def project_far_kernel(shift_ref, *refs, pieces, slots, counts, columns):
    total = sum(counts)
    outs = refs[pieces + total : -3]
    rows, wide, sems = refs[-3:]
    loads, at = [], 0
    for i, piece in enumerate(refs[:pieces]):
        place = rows.at[pl.ds(at, piece.shape[0])]
        loads.append(pltpu.make_async_copy(piece, place, sems.at[i]))
        at += piece.shape[0]
    weight_loads, number = [], pieces
    for i, weights in enumerate(cut_by(counts, refs[pieces : pieces + total])):
        begin, at = i * columns, 0
        for weight in weights:
            place = wide.at[
                begin // 256, pl.ds(at, weight.shape[0]), pl.ds(begin % 256, columns)
            ]
            weight_loads.append((i, pltpu.make_async_copy(weight, place, sems.at[number])))
            at += weight.shape[0]
            number += 1
    for copy in loads:
        copy.start()
    for _, copy in weight_loads:
        copy.start()
    for copy in loads:
        copy.wait()
    for tile in range(4 * columns // 256):
        inside = [i for i in range(4) if i * columns // 256 == tile]
        for i, copy in weight_loads:
            if i in inside:
                copy.wait()
        product = jnp.dot(rows[...], wide[tile], preferred_element_type=jnp.float32)
        for i in inside:
            begin = i * columns % 256
            store_for(outs, shift_ref[0], slots[i], product[:, begin : begin + columns])


def project_far(columns, shift, pieces, parts_of, slots, stacked=False):
    weights = [part for slot in slots for part in parts_of[slot]]
    counts = tuple(len(parts_of[slot]) for slot in slots)
    count = sum(piece.shape[0] for piece in pieces)
    width = pieces[0].shape[1]
    return pl.pallas_call(
        functools.partial(
            project_far_kernel, pieces=len(pieces), slots=slots, counts=counts, columns=columns
        ),
        in_specs=[SMEM] + [FAR] * (len(pieces) + len(weights)),
        out_specs=[VMEM] * (1 if stacked else 4),
        out_shape=[jax.ShapeDtypeStruct((4, count, columns), jnp.bfloat16)]
        if stacked
        else [jax.ShapeDtypeStruct((count, columns), jnp.bfloat16)] * 4,
        scratch_shapes=[
            pltpu.VMEM((count, width), jnp.bfloat16),
            pltpu.VMEM((4 * columns // 256, width, 256), jnp.bfloat16),
            pltpu.SemaphoreType.DMA((len(pieces) + len(weights),)),
        ],
        cost_estimate=LONG,
        compiler_params=LIMIT,
    )(shift, *pieces, *weights)


def project(kernel, columns, shift, pieces, parts_of, slots, stacked=False, mark=False):
    weights = [part for slot in slots for part in parts_of[slot]]
    counts = tuple(len(parts_of[slot]) for slot in slots)
    count = sum(piece.shape[0] for piece in pieces)
    width = pieces[0].shape[1]
    scratch = [pltpu.VMEM((count, width), jnp.bfloat16)]
    return pl.pallas_call(
        functools.partial(kernel, pieces=len(pieces), slots=slots, counts=counts),
        in_specs=[SMEM] + [VMEM] * (len(pieces) + len(weights)),
        out_specs=[VMEM] * (1 + mark if stacked else 4),
        out_shape=[
            jax.ShapeDtypeStruct((4, count, columns), jnp.bfloat16),
            jax.ShapeDtypeStruct((8, HEAD), jnp.float32),
        ][: 1 + mark]
        if stacked
        else [jax.ShapeDtypeStruct((count, columns), jnp.bfloat16)] * 4,
        scratch_shapes=scratch,
        cost_estimate=BRIEF if mark else LONG,
        compiler_params=LIMIT,
    )(shift, *pieces, *weights)


def project_rest(x, pieces, halves, slot, stack):
    _, count, columns = stack.shape
    width = pieces[0].shape[1]
    return pl.pallas_call(
        functools.partial(project_rest_kernel, pieces=len(pieces), slot=slot),
        in_specs=[SMEM] + [VMEM] * (len(pieces) + 2) + [FAR],
        out_specs=FAR,
        out_shape=jax.ShapeDtypeStruct(stack.shape, stack.dtype),
        input_output_aliases={3 + len(pieces): 0},
        scratch_shapes=[
            pltpu.VMEM((count, width), jnp.bfloat16),
            pltpu.VMEM((count, columns), jnp.bfloat16),
            pltpu.SemaphoreType.DMA,
        ],
        cost_estimate=LONG,
        compiler_params=LIMIT,
    )(x, *pieces, *halves[slot], stack)


def exchange(stack, axis):
    return lax.all_to_all(stack, axis, 0, 0, tiled=True)


def sum_of(stack):
    return jnp.sum(stack.astype(jnp.float32), axis=0).astype(jnp.bfloat16)


def sum_over_y(parts):
    own, one, two, three = parts
    total = own.astype(jnp.float32)
    for k, part in ((1, one), (3, three), (2, two)):
        total = total + send(part, "y", k).astype(jnp.float32)
    return total.astype(jnp.bfloat16)


def gather_x(block):
    return block, send(block, "x", -1), send(block, "x", -2), send(block, "x", -3)


def attend_kernel(x_ref, z_ref, bound_ref, flag_ref, q_ref, *refs):
    early, late, out = refs[:4], refs[4:8], refs[8]
    kfull, vfull = refs[9:]
    x, z = x_ref[0], z_ref[0]
    c1, c2, c3 = bound_ref[0], bound_ref[1], bound_ref[2]
    for r in range(4):
        lane = lax.rem(x + r, 4)
        for group, offsets in ((early[r], EARLY), (late[r], LATE)):
            for i, offset in enumerate(offsets):
                place = 4 * lax.rem(z + offset, 8) + lane
                at = pl.ds(pl.multiple_of(place * BLOCK, BLOCK), BLOCK)
                kfull[at, :] = group[i * BLOCK : (i + 1) * BLOCK, :HEAD]
                vfull[at, :] = group[i * BLOCK : (i + 1) * BLOCK, HEAD:]

    def first(i):
        return jnp.where(i >= c3, c3, jnp.where(i >= c2, c2, jnp.where(i >= c1, c1, 0)))

    def one_block(index, carry):
        there = 2 * lax.rem(x + lax.div(index, 2), 4) + lax.rem(index, 2)
        base = (4 * there + x) * BLOCK
        mine = pl.ds(pl.multiple_of(index * BLOCK, BLOCK), BLOCK)
        spans = lax.div(base + BLOCK - first(base) + SPAN - 1, SPAN)
        alive = flag_ref[4 * there + x] == 0

        @pl.when(jnp.logical_not(alive))
        def _():
            out[mine, :] = jnp.zeros((BLOCK, HEAD), jnp.bfloat16)

        for n in range(1, LONGEST + 1):

            @pl.when(alive & (spans == n))
            def _():
                keys = n * SPAN
                low = jnp.maximum(base + BLOCK - keys, 0)
                window = pl.ds(pl.multiple_of(low, BLOCK), keys)
                q_at = lax.rem(there - z + 8, 8) * BLOCK
                query = q_ref[pl.ds(pl.multiple_of(q_at, BLOCK), BLOCK), :]
                score = lax.dot_general(
                    query,
                    kfull[window, :],
                    (((1,), (1,)), ((), ())),
                    preferred_element_type=jnp.float32,
                ) * (1.0 / math.sqrt(HEAD))
                row = base + lax.broadcasted_iota(jnp.int32, (BLOCK, 1), 0)
                begin = first(row)
                column = low + lax.broadcasted_iota(jnp.int32, (BLOCK, keys), 1)
                score = jnp.where((column <= row) & (column >= begin), score, -1e30)
                expo = jnp.exp(score - jnp.max(score, axis=-1, keepdims=True))
                norm = jnp.sum(expo, axis=-1, keepdims=True)
                mixed = jnp.dot(
                    expo.astype(jnp.bfloat16), vfull[window, :], preferred_element_type=jnp.float32
                )
                out[mine, :] = (mixed / norm).astype(jnp.bfloat16)

        return carry

    lax.fori_loop(0, 8, one_block, 0)


def attend(x, z, bounds, flags, query, early, late):
    rows = query.shape[0]
    return pl.pallas_call(
        attend_kernel,
        in_specs=[SMEM] * 4 + [VMEM] * 9,
        out_specs=VMEM,
        out_shape=jax.ShapeDtypeStruct((rows, HEAD), jnp.bfloat16),
        scratch_shapes=[pltpu.VMEM((4 * rows, HEAD), jnp.bfloat16)] * 2,
        cost_estimate=BRIEF,
        compiler_params=LIMIT,
    )(x, z, bounds, flags, query, *early, *late)


def place_kernel(y_ref, *refs):
    parts, out = refs[:4], refs[4]
    for s in range(4):
        x = lax.rem(y_ref[0] + 4 - s, 4)
        for t in range(2):
            at = pl.ds(pl.multiple_of((4 * t + x) * BLOCK, BLOCK), BLOCK)
            out[at, :] = parts[s][t * BLOCK : (t + 1) * BLOCK, :]


def place(y, parts):
    rows = 4 * parts[0].shape[0]
    return pl.pallas_call(
        place_kernel,
        in_specs=[SMEM] + [VMEM] * 4,
        out_specs=VMEM,
        out_shape=jax.ShapeDtypeStruct((rows, HEAD), jnp.bfloat16),
    )(y, *parts)


def local(hidden, w_qkv, segment_ids, exit_flags):
    x, y, z = (lax.axis_index(axis).astype(jnp.int32) for axis in ("x", "y", "z"))
    weights = w_qkv[0]
    segment = segment_ids[0]
    steps = jnp.arange(1, 4, dtype=jnp.int32)
    bounds = jnp.sum((segment[None, :] < steps[:, None]).astype(jnp.int32), axis=1)
    x, y, z = (index.reshape(1) for index in (x, y, z))
    shift = lax.rem(x - y + 4, 4)
    blocks = gather_z_ring(hidden[0])
    key_value = jnp.concatenate([weights[:, 1, :], weights[:, 2, :]], axis=1)
    kv_w = gather_x_ring(key_value, (bounds, shift), (blocks[2], blocks[6]))

    def pieces(offsets):
        return [piece for offset in offsets for piece in blocks[offset]]

    near = pieces(EARLY)
    stack, mark = project(project_kernel, 256, x, near, kv_w, (0, 1, 3), True, True)
    near = after(near, blocks[3], blocks[5])
    stack = project_rest(x, near, kv_w, 2, stack)
    own = after(weights[:, 0, :], mark, kv_w[2])
    q_w = [(part,) for part in gather_x_by_right(own, stack)]
    received = exchange(stack, "y")
    late_pieces = after(pieces(LATE), stack)
    late_parts = project_far(256, shift, late_pieces, kv_w, (0, 1, 3, 2))
    late = sum_over_y(late_parts)
    early = sum_of(received)
    q_w = after(q_w, late_parts[0], early)
    early = gather_x_by_right(early)
    (stack,) = project_far(128, x, pieces(range(8)), q_w, (0, 1, 3, 2), True)
    query = sum_of(exchange(after(stack, late, early[1], early[3]), "y"))
    mixed = attend(x, z, bounds, exit_flags[0], query, early, gather_x(late))
    quarter = mixed.shape[0] // 4
    moved = [
        lax.ppermute(
            mixed[s * quarter : (s + 1) * quarter],
            ("x", "y"),
            [(4 * i + j, 4 * j + (i + s) % 4) for i in range(4) for j in range(4)],
        )
        for s in range(4)
    ]
    result = place(y, moved)
    handed = send(result, "phase", 1)
    return (result[None], handed[None])


def solution(mesh):
    split = Mesh(mesh.devices.reshape(2, 8, 4, 4), ("phase", "z", "x", "y"))
    tok = ("z", "x")
    in_specs = (
        P("phase", tok, "y"),
        P("phase", "y", None, tok),
        P("phase", None),
        P("phase", None),
    )
    out_specs = (P("phase", "y", tok), P("phase", "y", tok))
    return jax.shard_map(local, mesh=split, in_specs=in_specs, out_specs=out_specs, check_vma=False)
```

```python
import functools
import math

import jax
import jax.numpy as jnp
from jax import lax
from jax.experimental import pallas as pl
from jax.experimental.pallas import tpu as pltpu
from jax.sharding import Mesh
from jax.sharding import PartitionSpec as P

HEAD = 128
BLOCK = 128
SPAN = 256
LONGEST = 9
EARLY = (0, 1, 2, 6, 7)
LATE = (3, 4, 5)
CUT = 896
BRIEF = pl.CostEstimate(flops=1, bytes_accessed=1, transcendentals=0)
LONG = pl.CostEstimate(flops=3 * 10**10, bytes_accessed=1, transcendentals=0)
VMEM = pl.BlockSpec(memory_space=pltpu.VMEM)
FAR = pl.BlockSpec(memory_space=pltpu.HBM)
SMEM = pl.BlockSpec(memory_space=pltpu.SMEM)
LIMIT = pltpu.CompilerParams(vmem_limit_bytes=32 * 2**20)


def send(block, axis, distance):
    n = lax.axis_size(axis)
    return lax.ppermute(block, axis, [(i, (i + distance) % n) for i in range(n)])


def after(values, *earlier):
    return lax.optimization_barrier((values, earlier))[0]


def gather_x_ring(part, earlier, second):
    left = send(part, "x", 1)
    right = send(part, "x", -1)
    top = send(after(right, earlier)[:CUT], "x", -1)
    bottom = send(after(left, second)[CUT:], "x", 1)
    return {0: (part,), 1: (right,), 3: (left,), 2: (top, bottom)}


def gather_x_by_right(block, *earlier):
    right = send(block, "x", -1)
    return block, right, send(after(right, earlier), "x", -1), send(block, "x", 1)


def gather_z_ring(block):
    found = {0: [block]}
    left = right = block
    for step in (1, 2, 3):
        left, right = send(left, "z", 1), send(right, "z", -1)
        found[8 - step], found[step] = [left], [right]
    found[4] = [send(left, "z", 1)]
    return found


def loads_of(pieces, weights, columns, rows, wide, sems):
    row_loads, at = [], 0
    for i, piece in enumerate(pieces):
        place = rows.at[pl.ds(at, piece.shape[0])]
        row_loads.append(pltpu.make_async_copy(piece, place, sems.at[i]))
        at += piece.shape[0]
    slot_loads, number = [], len(pieces)
    for i, parts in enumerate(weights):
        begin, at, copies = i * columns, 0, []
        for part in parts:
            place = wide.at[begin // 256, pl.ds(at, part.shape[0]), pl.ds(begin % 256, columns)]
            copies.append(pltpu.make_async_copy(part, place, sems.at[number]))
            at += part.shape[0]
            number += 1
        slot_loads.append(copies)
    for copies in [row_loads] + slot_loads:
        for copy in copies:
            copy.start()
    for copy in row_loads:
        copy.wait()
    return slot_loads


def cut_by(counts, refs):
    groups, at = [], 0
    for count in counts:
        groups.append(refs[at : at + count])
        at += count
    return groups


def products(pieces, weights, columns, rows, wide, sems):
    slot_loads = loads_of(pieces, weights, columns, rows, wide, sems)
    per_tile = 256 // columns
    for tile in range(len(weights) // per_tile):
        inside = range(tile * per_tile, (tile + 1) * per_tile)
        for i in inside:
            for copy in slot_loads[i]:
                copy.wait()
        product = jnp.dot(rows[...], wide[tile], preferred_element_type=jnp.float32)
        for i in inside:
            begin = i * columns % 256
            yield i, product[:, begin : begin + columns].astype(jnp.bfloat16)


def scratch_for(count, width, columns, slots, operands):
    return [
        pltpu.VMEM((count, width), jnp.bfloat16),
        pltpu.VMEM((slots * columns // 256, width, 256), jnp.bfloat16),
        pltpu.SemaphoreType.DMA((operands,)),
    ]


def project_kernel(shift_ref, *refs, pieces, slots, counts, columns):
    total = pieces + sum(counts)
    outs = refs[total : total + 4]
    weights = cut_by(counts, refs[pieces:total])
    for i, product in products(refs[:pieces], weights, columns, *refs[total + 4 :]):
        target = lax.rem(slots[i] + shift_ref[0], 4)
        for k in range(4):

            @pl.when(target == k)
            def _():
                outs[k][...] = product


def project_stack_kernel(x_ref, *refs, pieces, slots, counts, columns, added):
    total = pieces + sum(counts)
    weights = cut_by(counts, refs[pieces:total])
    out, mark = refs[total + added : total + added + 2]
    rows, wide, sems, stage, out_sems = refs[total + added + 2 :]
    mark[...] = jnp.zeros_like(mark)
    copies = []
    for i, product in products(refs[:pieces], weights, columns, rows, wide, sems):
        stage[i] = product
        place = out.at[lax.rem(slots[i] + x_ref[0], 4)]
        copies.append(pltpu.make_async_copy(stage.at[i], place, out_sems.at[i]))
        copies[-1].start()
    for copy in copies:
        copy.wait()


def project(columns, shift, pieces, parts_of, slots):
    weights = [part for slot in slots for part in parts_of[slot]]
    counts = tuple(len(parts_of[slot]) for slot in slots)
    count = sum(piece.shape[0] for piece in pieces)
    width = pieces[0].shape[1]
    operands = len(pieces) + len(weights)
    return pl.pallas_call(
        functools.partial(
            project_kernel, pieces=len(pieces), slots=slots, counts=counts, columns=columns
        ),
        in_specs=[SMEM] + [FAR] * operands,
        out_specs=[VMEM] * 4,
        out_shape=[jax.ShapeDtypeStruct((count, columns), jnp.bfloat16)] * 4,
        scratch_shapes=scratch_for(count, width, columns, len(slots), operands),
        cost_estimate=LONG,
        compiler_params=LIMIT,
    )(shift, *pieces, *weights)


def project_stack(columns, x, pieces, parts_of, slots, stack=None):
    weights = [part for slot in slots for part in parts_of[slot]]
    counts = tuple(len(parts_of[slot]) for slot in slots)
    count = sum(piece.shape[0] for piece in pieces)
    width = pieces[0].shape[1]
    operands = len(pieces) + len(weights)
    extra = [] if stack is None else [stack]
    return pl.pallas_call(
        functools.partial(
            project_stack_kernel,
            pieces=len(pieces),
            slots=slots,
            counts=counts,
            columns=columns,
            added=len(extra),
        ),
        in_specs=[SMEM] + [FAR] * (operands + len(extra)),
        out_specs=[FAR, VMEM],
        out_shape=[
            jax.ShapeDtypeStruct((4, count, columns), jnp.bfloat16),
            jax.ShapeDtypeStruct((8, HEAD), jnp.float32),
        ],
        input_output_aliases={1 + operands: 0} if extra else {},
        scratch_shapes=scratch_for(count, width, columns, len(slots), operands)
        + [
            pltpu.VMEM((len(slots), count, columns), jnp.bfloat16),
            pltpu.SemaphoreType.DMA((len(slots),)),
        ],
        cost_estimate=BRIEF if len(slots) == 3 else LONG,
        compiler_params=LIMIT,
    )(x, *pieces, *weights, *extra)


def exchange(stack, axis):
    return lax.all_to_all(stack, axis, 0, 0, tiled=True)


def sum_of(stack):
    return jnp.sum(stack.astype(jnp.float32), axis=0).astype(jnp.bfloat16)


def sum_over_y(parts, *earlier):
    received = after([send(part, "y", k) for k, part in enumerate(parts) if k], earlier)
    total = parts[0].astype(jnp.float32)
    for part in received:
        total = total + part.astype(jnp.float32)
    return total.astype(jnp.bfloat16)


def gather_x(block):
    return block, send(block, "x", -1), send(block, "x", -2), send(block, "x", -3)


def attend_kernel(x_ref, z_ref, bound_ref, flag_ref, q_ref, *refs):
    early, late, out = refs[:4], refs[4:8], refs[8]
    kfull, vfull = refs[9:]
    x, z = x_ref[0], z_ref[0]
    c1, c2, c3 = bound_ref[0], bound_ref[1], bound_ref[2]
    for r in range(4):
        lane = lax.rem(x + r, 4)
        for group, offsets in ((early[r], EARLY), (late[r], LATE)):
            for i, offset in enumerate(offsets):
                place = 4 * lax.rem(z + offset, 8) + lane
                at = pl.ds(pl.multiple_of(place * BLOCK, BLOCK), BLOCK)
                kfull[at, :] = group[i * BLOCK : (i + 1) * BLOCK, :HEAD]
                vfull[at, :] = group[i * BLOCK : (i + 1) * BLOCK, HEAD:]

    def first(i):
        return jnp.where(i >= c3, c3, jnp.where(i >= c2, c2, jnp.where(i >= c1, c1, 0)))

    def one_block(index, carry):
        there = 2 * lax.rem(x + lax.div(index, 2), 4) + lax.rem(index, 2)
        base = (4 * there + x) * BLOCK
        mine = pl.ds(pl.multiple_of(index * BLOCK, BLOCK), BLOCK)
        spans = lax.div(base + BLOCK - first(base) + SPAN - 1, SPAN)
        alive = flag_ref[4 * there + x] == 0

        @pl.when(jnp.logical_not(alive))
        def _():
            out[mine, :] = jnp.zeros((BLOCK, HEAD), jnp.bfloat16)

        for n in range(1, LONGEST + 1):

            @pl.when(alive & (spans == n))
            def _():
                keys = n * SPAN
                low = jnp.maximum(base + BLOCK - keys, 0)
                window = pl.ds(pl.multiple_of(low, BLOCK), keys)
                q_at = lax.rem(there - z + 8, 8) * BLOCK
                query = q_ref[pl.ds(pl.multiple_of(q_at, BLOCK), BLOCK), :]
                score = lax.dot_general(
                    query,
                    kfull[window, :],
                    (((1,), (1,)), ((), ())),
                    preferred_element_type=jnp.float32,
                ) * (1.0 / math.sqrt(HEAD))
                row = base + lax.broadcasted_iota(jnp.int32, (BLOCK, 1), 0)
                begin = first(row)
                column = low + lax.broadcasted_iota(jnp.int32, (BLOCK, keys), 1)
                score = jnp.where((column <= row) & (column >= begin), score, -1e30)
                expo = jnp.exp(score - jnp.max(score, axis=-1, keepdims=True))
                norm = jnp.sum(expo, axis=-1, keepdims=True)
                mixed = jnp.dot(
                    expo.astype(jnp.bfloat16), vfull[window, :], preferred_element_type=jnp.float32
                )
                out[mine, :] = (mixed / norm).astype(jnp.bfloat16)

        return carry

    lax.fori_loop(0, 8, one_block, 0)


def attend(x, z, bounds, flags, query, early, late):
    rows = query.shape[0]
    return pl.pallas_call(
        attend_kernel,
        in_specs=[SMEM] * 4 + [VMEM] * 9,
        out_specs=VMEM,
        out_shape=jax.ShapeDtypeStruct((rows, HEAD), jnp.bfloat16),
        scratch_shapes=[pltpu.VMEM((4 * rows, HEAD), jnp.bfloat16)] * 2,
        cost_estimate=BRIEF,
        compiler_params=LIMIT,
    )(x, z, bounds, flags, query, *early, *late)


def place_kernel(y_ref, *refs):
    parts, outs = refs[:4], refs[4:]
    for s in range(4):
        x = lax.rem(y_ref[0] + 4 - s, 4)
        for t in range(2):
            at = pl.ds(pl.multiple_of((4 * t + x) * BLOCK, BLOCK), BLOCK)
            for out in outs:
                out[at, :] = parts[s][t * BLOCK : (t + 1) * BLOCK, :]


def place(y, parts):
    rows = 4 * parts[0].shape[0]
    return pl.pallas_call(
        place_kernel,
        in_specs=[SMEM] + [VMEM] * 4,
        out_specs=[VMEM] * 2,
        out_shape=[jax.ShapeDtypeStruct((rows, HEAD), jnp.bfloat16)] * 2,
    )(y, *parts)


def local(hidden, w_qkv, segment_ids, exit_flags):
    x, y, z = (lax.axis_index(axis).astype(jnp.int32) for axis in ("x", "y", "z"))
    weights = w_qkv[0]
    segment = segment_ids[0]
    steps = jnp.arange(1, 4, dtype=jnp.int32)
    bounds = jnp.sum((segment[None, :] < steps[:, None]).astype(jnp.int32), axis=1)
    x, y, z = (index.reshape(1) for index in (x, y, z))
    shift = lax.rem(x - y + 4, 4)
    blocks = gather_z_ring(hidden[0])
    key_value = jnp.concatenate([weights[:, 1, :], weights[:, 2, :]], axis=1)
    kv_w = gather_x_ring(key_value, (bounds, shift), (blocks[2], blocks[6]))

    def pieces(offsets):
        return [piece for offset in offsets for piece in blocks[offset]]

    near = pieces(EARLY)
    stack, mark = project_stack(256, x, near, kv_w, (0, 1, 3))
    near = after(near, blocks[3], blocks[5])
    own = after(weights[:, 0, :], mark, kv_w[2])
    stack, mark = project_stack(256, x, near, kv_w, (2,), stack)
    q_w = [(part,) for part in gather_x_by_right(own)]
    received = exchange(stack, "y")
    late_parts = project(256, shift, after(pieces(LATE), mark), kv_w, (0, 1, 3, 2))
    early = sum_of(received)
    q_w = after(q_w, late_parts[0], early)
    early = gather_x_by_right(early)
    stack, mark = project_stack(128, x, pieces(range(8)), q_w, (0, 1, 3, 2))
    late = sum_over_y(late_parts, stack)
    query = sum_of(exchange(after(stack, late, early[1], early[3]), "y"))
    mixed = attend(x, z, bounds, exit_flags[0], query, early, gather_x(late))
    quarter = mixed.shape[0] // 4
    moved = [
        lax.ppermute(
            mixed[s * quarter : (s + 1) * quarter],
            ("x", "y"),
            [(4 * i + j, 4 * j + (i + s) % 4) for i in range(4) for j in range(4)],
        )
        for s in range(4)
    ]
    result, given = place(y, moved)
    handed = send(given, "phase", 1)
    return (result[None], handed[None])


def solution(mesh):
    split = Mesh(mesh.devices.reshape(2, 8, 4, 4), ("phase", "z", "x", "y"))
    tok = ("z", "x")
    in_specs = (
        P("phase", tok, "y"),
        P("phase", "y", None, tok),
        P("phase", None),
        P("phase", None),
    )
    out_specs = (P("phase", "y", tok), P("phase", "y", tok))
    return jax.shard_map(local, mesh=split, in_specs=in_specs, out_specs=out_specs, check_vma=False)
```

```python
import functools
import math

import jax
import jax.numpy as jnp
from jax import lax
from jax.experimental import pallas as pl
from jax.experimental.pallas import tpu as pltpu
from jax.sharding import Mesh
from jax.sharding import PartitionSpec as P

HEAD = 128
BLOCK = 128
SPAN = 256
LONGEST = 9
EARLY = (0, 1, 2, 6, 7)
LATE = (3, 4, 5)
CUT = 896
BRIEF = pl.CostEstimate(flops=1, bytes_accessed=1, transcendentals=0)
LONG = pl.CostEstimate(flops=3 * 10**10, bytes_accessed=1, transcendentals=0)
VMEM = pl.BlockSpec(memory_space=pltpu.VMEM)
FAR = pl.BlockSpec(memory_space=pl.ANY)
SMEM = pl.BlockSpec(memory_space=pltpu.SMEM)
LIMIT = pltpu.CompilerParams(vmem_limit_bytes=32 * 2**20)


def send(block, axis, distance):
    n = lax.axis_size(axis)
    return lax.ppermute(block, axis, [(i, (i + distance) % n) for i in range(n)])


def after(values, *earlier):
    return lax.optimization_barrier((values, earlier))[0]


def gather_x_ring(part, earlier, second):
    left = send(part, "x", 1)
    right = send(part, "x", -1)
    top = send(after(right, earlier)[:CUT], "x", -1)
    bottom = send(after(left, second)[CUT:], "x", 1)
    return {0: (part,), 1: (right,), 3: (left,), 2: (top, bottom)}


def gather_x_by_right(block, *earlier):
    right = send(block, "x", -1)
    return block, right, send(after(right, earlier), "x", -1), send(block, "x", 1)


def gather_z_ring(block):
    found = {0: [block]}
    left = right = block
    for step in (1, 2, 3):
        left, right = send(left, "z", 1), send(right, "z", -1)
        found[8 - step], found[step] = [left], [right]
    found[4] = [send(left, "z", 1)]
    return found


def loads_of(pieces, weights, columns, rows, wide, sems):
    row_loads, at = [], 0
    for i, piece in enumerate(pieces):
        place = rows.at[pl.ds(at, piece.shape[0])]
        row_loads.append(pltpu.make_async_copy(piece, place, sems.at[i]))
        at += piece.shape[0]
    slot_loads, number = [], len(pieces)
    for i, parts in enumerate(weights):
        begin, at, copies = i * columns, 0, []
        for part in parts:
            place = wide.at[begin // 256, pl.ds(at, part.shape[0]), pl.ds(begin % 256, columns)]
            copies.append(pltpu.make_async_copy(part, place, sems.at[number]))
            at += part.shape[0]
            number += 1
        slot_loads.append(copies)
    for copies in [row_loads] + slot_loads:
        for copy in copies:
            copy.start()
    return row_loads, slot_loads


def cut_by(counts, refs):
    groups, at = [], 0
    for count in counts:
        groups.append(refs[at : at + count])
        at += count
    return groups


def products(pieces, weights, columns, rows, wide, sems):
    row_loads, slot_loads = loads_of(pieces, weights, columns, rows, wide, sems)
    per_tile = 256 // columns
    cut = 4 if len(pieces) == 8 else len(pieces)
    middle = sum(piece.shape[0] for piece in pieces[:cut])
    parts = [(slice(0, middle), row_loads[:cut])]
    if middle < rows.shape[0]:
        parts.append((slice(middle, rows.shape[0]), row_loads[cut:]))
    for tile in range(len(weights) // per_tile):
        inside = range(tile * per_tile, (tile + 1) * per_tile)
        for i in inside:
            for copy in slot_loads[i]:
                copy.wait()
        for part, copies in parts:
            if tile == 0:
                for copy in copies:
                    copy.wait()
            product = jnp.dot(rows[part, :], wide[tile], preferred_element_type=jnp.float32)
            last = part.stop == rows.shape[0]
            for i in inside:
                begin = i * columns % 256
                value = product[:, begin : begin + columns].astype(jnp.bfloat16)
                yield i, part, last, value


def scratch_for(count, width, columns, slots, operands):
    return [
        pltpu.VMEM((count, width), jnp.bfloat16),
        pltpu.VMEM((slots * columns // 256, width, 256), jnp.bfloat16),
        pltpu.SemaphoreType.DMA((operands,)),
    ]


def project_kernel(shift_ref, *refs, pieces, slots, counts, columns):
    total = pieces + sum(counts)
    outs = refs[total : total + 4]
    weights = cut_by(counts, refs[pieces:total])
    rows, wide, sems, stage, out_sems = refs[total + 4 :]

    def for_target(i, act):
        target = lax.rem(slots[i] + shift_ref[0], 4)
        for k in range(4):

            @pl.when(target == k)
            def _():
                act(pltpu.make_async_copy(stage.at[i], outs[k], out_sems.at[i]))

    for i, part, last, value in products(refs[:pieces], weights, columns, rows, wide, sems):
        stage[i, part, :] = value
        if last:
            for_target(i, lambda copy: copy.start())
    for i in range(4):
        for_target(i, lambda copy: copy.wait())


def project_stack_kernel(x_ref, *refs, pieces, slots, counts, columns, added):
    total = pieces + sum(counts)
    weights = cut_by(counts, refs[pieces:total])
    out, mark = refs[total + added : total + added + 2]
    rows, wide, sems, stage, out_sems = refs[total + added + 2 :]
    mark[...] = jnp.zeros_like(mark)
    copies = []
    for i, part, last, value in products(refs[:pieces], weights, columns, rows, wide, sems):
        stage[i, part, :] = value
        if not last:
            continue
        place = out.at[lax.rem(slots[i] + x_ref[0], 4)]
        copies.append(pltpu.make_async_copy(stage.at[i], place, out_sems.at[i]))
        copies[-1].start()
    for copy in copies:
        copy.wait()


def project(columns, shift, pieces, parts_of, slots):
    weights = [part for slot in slots for part in parts_of[slot]]
    counts = tuple(len(parts_of[slot]) for slot in slots)
    count = sum(piece.shape[0] for piece in pieces)
    width = pieces[0].shape[1]
    operands = len(pieces) + len(weights)
    return pl.pallas_call(
        functools.partial(
            project_kernel, pieces=len(pieces), slots=slots, counts=counts, columns=columns
        ),
        in_specs=[SMEM] + [FAR] * operands,
        out_specs=[FAR] * 4,
        out_shape=[jax.ShapeDtypeStruct((count, columns), jnp.bfloat16)] * 4,
        scratch_shapes=scratch_for(count, width, columns, len(slots), operands)
        + [
            pltpu.VMEM((len(slots), count, columns), jnp.bfloat16),
            pltpu.SemaphoreType.DMA((len(slots),)),
        ],
        cost_estimate=LONG,
        compiler_params=LIMIT,
    )(shift, *pieces, *weights)


def project_stack(columns, x, pieces, parts_of, slots, stack=None):
    weights = [part for slot in slots for part in parts_of[slot]]
    counts = tuple(len(parts_of[slot]) for slot in slots)
    count = sum(piece.shape[0] for piece in pieces)
    width = pieces[0].shape[1]
    operands = len(pieces) + len(weights)
    extra = [] if stack is None else [stack]
    return pl.pallas_call(
        functools.partial(
            project_stack_kernel,
            pieces=len(pieces),
            slots=slots,
            counts=counts,
            columns=columns,
            added=len(extra),
        ),
        in_specs=[SMEM] + [FAR] * (operands + len(extra)),
        out_specs=[FAR, VMEM],
        out_shape=[
            jax.ShapeDtypeStruct((4, count, columns), jnp.bfloat16),
            jax.ShapeDtypeStruct((8, HEAD), jnp.float32),
        ],
        input_output_aliases={1 + operands: 0} if extra else {},
        scratch_shapes=scratch_for(count, width, columns, len(slots), operands)
        + [
            pltpu.VMEM((len(slots), count, columns), jnp.bfloat16),
            pltpu.SemaphoreType.DMA((len(slots),)),
        ],
        cost_estimate=BRIEF if len(slots) == 3 else LONG,
        compiler_params=LIMIT,
    )(x, *pieces, *weights, *extra)


def exchange(stack, axis):
    return lax.all_to_all(stack, axis, 0, 0, tiled=True)


def sum_of(stack):
    return jnp.sum(stack.astype(jnp.float32), axis=0).astype(jnp.bfloat16)


def sum_over_y(parts, *earlier):
    received = after([send(part, "y", k) for k, part in enumerate(parts) if k], earlier)
    total = parts[0].astype(jnp.float32)
    for part in received:
        total = total + part.astype(jnp.float32)
    return total.astype(jnp.bfloat16)


def gather_x(block):
    return block, send(block, "x", -1), send(block, "x", -2), send(block, "x", -3)


def attend_kernel(x_ref, z_ref, bound_ref, flag_ref, q_ref, *refs):
    early, late, out = refs[:4], refs[4:8], refs[8]
    kfull, vfull = refs[9:]
    x, z = x_ref[0], z_ref[0]
    c1, c2, c3 = bound_ref[0], bound_ref[1], bound_ref[2]
    for r in range(4):
        lane = lax.rem(x + r, 4)
        for group, offsets in ((early[r], EARLY), (late[r], LATE)):
            for i, offset in enumerate(offsets):
                place = 4 * lax.rem(z + offset, 8) + lane
                at = pl.ds(pl.multiple_of(place * BLOCK, BLOCK), BLOCK)
                kfull[at, :] = group[i * BLOCK : (i + 1) * BLOCK, :HEAD]
                vfull[at, :] = group[i * BLOCK : (i + 1) * BLOCK, HEAD:]

    def first(i):
        return jnp.where(i >= c3, c3, jnp.where(i >= c2, c2, jnp.where(i >= c1, c1, 0)))

    def one_block(index, carry):
        there = 2 * lax.rem(x + lax.div(index, 2), 4) + lax.rem(index, 2)
        base = (4 * there + x) * BLOCK
        mine = pl.ds(pl.multiple_of(index * BLOCK, BLOCK), BLOCK)
        spans = lax.div(base + BLOCK - first(base) + SPAN - 1, SPAN)
        alive = flag_ref[4 * there + x] == 0

        @pl.when(jnp.logical_not(alive))
        def _():
            out[mine, :] = jnp.zeros((BLOCK, HEAD), jnp.bfloat16)

        for n in range(1, LONGEST + 1):

            @pl.when(alive & (spans == n))
            def _():
                keys = n * SPAN
                low = jnp.maximum(base + BLOCK - keys, 0)
                window = pl.ds(pl.multiple_of(low, BLOCK), keys)
                q_at = lax.rem(there - z + 8, 8) * BLOCK
                query = q_ref[pl.ds(pl.multiple_of(q_at, BLOCK), BLOCK), :]
                score = lax.dot_general(
                    query,
                    kfull[window, :],
                    (((1,), (1,)), ((), ())),
                    preferred_element_type=jnp.float32,
                ) * (1.0 / math.sqrt(HEAD))
                row = base + lax.broadcasted_iota(jnp.int32, (BLOCK, 1), 0)
                begin = first(row)
                column = low + lax.broadcasted_iota(jnp.int32, (BLOCK, keys), 1)
                score = jnp.where((column <= row) & (column >= begin), score, -1e30)
                expo = jnp.exp(score - jnp.max(score, axis=-1, keepdims=True))
                norm = jnp.sum(expo, axis=-1, keepdims=True)
                mixed = jnp.dot(
                    expo.astype(jnp.bfloat16), vfull[window, :], preferred_element_type=jnp.float32
                )
                out[mine, :] = (mixed / norm).astype(jnp.bfloat16)

        return carry

    lax.fori_loop(0, 8, one_block, 0)


def attend(x, z, bounds, flags, query, early, late):
    rows = query.shape[0]
    return pl.pallas_call(
        attend_kernel,
        in_specs=[SMEM] * 4 + [VMEM] * 9,
        out_specs=VMEM,
        out_shape=jax.ShapeDtypeStruct((rows, HEAD), jnp.bfloat16),
        scratch_shapes=[pltpu.VMEM((4 * rows, HEAD), jnp.bfloat16)] * 2,
        cost_estimate=BRIEF,
        compiler_params=pltpu.CompilerParams(vmem_limit_bytes=24 * 2**20),
    )(x, z, bounds, flags, query, *early, *late)


def place_kernel(y_ref, *refs):
    parts, outs, whole, sems = refs[:4], refs[4:6], refs[6], refs[7]
    loads = []
    for s in range(4):
        x = lax.rem(y_ref[0] + 4 - s, 4)
        for t in range(2):
            at = pl.ds(pl.multiple_of((4 * t + x) * BLOCK, BLOCK), BLOCK)
            source = parts[s].at[pl.ds(t * BLOCK, BLOCK)]
            loads.append(pltpu.make_async_copy(source, whole.at[at], sems.at[2 + len(loads)]))
    for copy in loads:
        copy.start()
    for copy in loads:
        copy.wait()
    copies = [pltpu.make_async_copy(whole, out, sems.at[i]) for i, out in enumerate(outs)]
    for copy in copies:
        copy.start()
    for copy in copies:
        copy.wait()


def place(y, parts):
    rows = 4 * parts[0].shape[0]
    return pl.pallas_call(
        place_kernel,
        in_specs=[SMEM] + [FAR] * 4,
        out_specs=[FAR] * 2,
        out_shape=[jax.ShapeDtypeStruct((rows, HEAD), jnp.bfloat16)] * 2,
        scratch_shapes=[
            pltpu.VMEM((rows, HEAD), jnp.bfloat16),
            pltpu.SemaphoreType.DMA((10,)),
        ],
        compiler_params=pltpu.CompilerParams(vmem_limit_bytes=58 * 2**20),
    )(y, *parts)


def local(hidden, w_qkv, segment_ids, exit_flags):
    x, y, z = (lax.axis_index(axis).astype(jnp.int32) for axis in ("x", "y", "z"))
    weights = w_qkv[0]
    segment = segment_ids[0]
    steps = jnp.arange(1, 4, dtype=jnp.int32)
    bounds = jnp.sum((segment[None, :] < steps[:, None]).astype(jnp.int32), axis=1)
    x, y, z = (index.reshape(1) for index in (x, y, z))
    shift = lax.rem(x - y + 4, 4)
    blocks = gather_z_ring(hidden[0])
    key_value = jnp.concatenate([weights[:, 1, :], weights[:, 2, :]], axis=1)
    kv_w = gather_x_ring(key_value, (bounds, shift), (blocks[2], blocks[6]))

    def pieces(offsets):
        return [piece for offset in offsets for piece in blocks[offset]]

    near = pieces(EARLY)
    stack, mark = project_stack(256, x, near, kv_w, (0, 1, 3))
    near = after(near, blocks[3], blocks[5])
    own = after(weights[:, 0, :], mark, kv_w[2])
    stack, mark = project_stack(256, x, near, kv_w, (2,), stack)
    q_w = [(part,) for part in gather_x_by_right(own)]
    received = exchange(stack, "y")
    late_parts = project(256, shift, after(pieces(LATE), mark), kv_w, (0, 1, 3, 2))
    early = sum_of(received)
    q_w = after(q_w, late_parts[0], early)
    early = gather_x_by_right(early)
    stack, mark = project_stack(128, x, pieces(range(8)), q_w, (0, 1, 3, 2))
    late = sum_over_y(late_parts, stack)
    query = sum_of(exchange(after(stack, late, early[1], early[3]), "y"))
    mixed = attend(x, z, bounds, exit_flags[0], query, early, gather_x(late))
    quarter = mixed.shape[0] // 4
    moved = [
        lax.ppermute(
            mixed[s * quarter : (s + 1) * quarter],
            ("x", "y"),
            [(4 * i + j, 4 * j + (i + s) % 4) for i in range(4) for j in range(4)],
        )
        for s in range(4)
    ]
    result, given = place(y, moved)
    handed = send(given[None], "phase", 1)
    return (result[None], handed)


def solution(mesh):
    split = Mesh(mesh.devices.reshape(2, 8, 4, 4), ("phase", "z", "x", "y"))
    tok = ("z", "x")
    in_specs = (
        P("phase", tok, "y"),
        P("phase", "y", None, tok),
        P("phase", None),
        P("phase", None),
    )
    out_specs = (P("phase", "y", tok), P("phase", "y", tok))
    return jax.shard_map(local, mesh=split, in_specs=in_specs, out_specs=out_specs, check_vma=False)
```

```python
import functools
import math

import jax
import jax.numpy as jnp
from jax import lax
from jax.experimental import pallas as pl
from jax.experimental.pallas import tpu as pltpu
from jax.sharding import Mesh
from jax.sharding import PartitionSpec as P

HEAD = 128
BLOCK = 128
SPAN = 256
LONGEST = 9
EARLY = (0, 1, 2, 6, 7)
LATE = (3, 4, 5)
CUT = 896
BRIEF = pl.CostEstimate(flops=1, bytes_accessed=1, transcendentals=0)
LONG = pl.CostEstimate(flops=3 * 10**10, bytes_accessed=1, transcendentals=0)
VMEM = pl.BlockSpec(memory_space=pltpu.VMEM)
FAR = pl.BlockSpec(memory_space=pl.ANY)
SMEM = pl.BlockSpec(memory_space=pltpu.SMEM)
LIMIT = pltpu.CompilerParams(vmem_limit_bytes=58 * 2**20)


def send(block, axis, distance):
    n = lax.axis_size(axis)
    return lax.ppermute(block, axis, [(i, (i + distance) % n) for i in range(n)])


def after(values, *earlier):
    return lax.optimization_barrier((values, earlier))[0]


def gather_x_ring(part, earlier, second):
    left = send(part, "x", 1)
    right = send(part, "x", -1)
    top = send(after(right, earlier)[:CUT], "x", -1)
    bottom = send(after(left, second)[CUT:], "x", 1)
    return {0: (part,), 1: (right,), 3: (left,), 2: (top, bottom)}


def gather_x_by_right(block, *earlier):
    right = send(block, "x", -1)
    return block, right, send(after(right, earlier), "x", -1), send(block, "x", 1)


def gather_z_ring(block):
    found = {0: [block]}
    left = right = block
    for step in (1, 2, 3):
        left, right = send(left, "z", 1), send(right, "z", -1)
        found[8 - step], found[step] = [left], [right]
    found[4] = [send(left, "z", 1)]
    return found


def loads_of(pieces, weights, columns, rows, wide, sems):
    row_loads, at = [], 0
    for i, piece in enumerate(pieces):
        place = rows.at[pl.ds(at, piece.shape[0])]
        row_loads.append(pltpu.make_async_copy(piece, place, sems.at[i]))
        at += piece.shape[0]
    slot_loads, number = [], len(pieces)
    for i, parts in enumerate(weights):
        begin, at, copies = i * columns, 0, []
        for part in parts:
            place = wide.at[begin // 256, pl.ds(at, part.shape[0]), pl.ds(begin % 256, columns)]
            copies.append(pltpu.make_async_copy(part, place, sems.at[number]))
            at += part.shape[0]
            number += 1
        slot_loads.append(copies)
    for copies in [row_loads] + slot_loads:
        for copy in copies:
            copy.start()
    return row_loads, slot_loads


def cut_by(counts, refs):
    groups, at = [], 0
    for count in counts:
        groups.append(refs[at : at + count])
        at += count
    return groups


def products(pieces, weights, columns, rows, wide, sems):
    row_loads, slot_loads = loads_of(pieces, weights, columns, rows, wide, sems)
    per_tile = 256 // columns
    cut = 4 if len(pieces) == 8 else len(pieces)
    middle = sum(piece.shape[0] for piece in pieces[:cut])
    parts = [(slice(0, middle), row_loads[:cut])]
    if middle < rows.shape[0]:
        parts.append((slice(middle, rows.shape[0]), row_loads[cut:]))
    for tile in range(len(weights) // per_tile):
        inside = range(tile * per_tile, (tile + 1) * per_tile)
        for i in inside:
            for copy in slot_loads[i]:
                copy.wait()
        for part, copies in parts:
            if tile == 0:
                for copy in copies:
                    copy.wait()
            product = jnp.dot(rows[part, :], wide[tile], preferred_element_type=jnp.float32)
            last = part.stop == rows.shape[0]
            for i in inside:
                begin = i * columns % 256
                value = product[:, begin : begin + columns].astype(jnp.bfloat16)
                yield i, part, last, value


def scratch_for(count, width, columns, slots, operands):
    return [
        pltpu.VMEM((count, width), jnp.bfloat16),
        pltpu.VMEM((slots * columns // 256, width, 256), jnp.bfloat16),
        pltpu.SemaphoreType.DMA((operands,)),
    ]


def project_kernel(shift_ref, *refs, pieces, slots, counts, columns):
    total = pieces + sum(counts)
    outs = refs[total : total + 4]
    weights = cut_by(counts, refs[pieces:total])
    rows, wide, sems, stage, out_sems = refs[total + 4 :]

    def for_target(i, act):
        target = lax.rem(slots[i] + shift_ref[0], 4)
        for k in range(4):

            @pl.when(target == k)
            def _():
                act(pltpu.make_async_copy(stage.at[i], outs[k], out_sems.at[i]))

    for i, part, last, value in products(refs[:pieces], weights, columns, rows, wide, sems):
        stage[i, part, :] = value
        if last:
            for_target(i, lambda copy: copy.start())
    for i in range(4):
        for_target(i, lambda copy: copy.wait())


def project_stack_kernel(x_ref, *refs, pieces, slots, counts, columns, added):
    total = pieces + sum(counts)
    weights = cut_by(counts, refs[pieces:total])
    out, mark = refs[total + added : total + added + 2]
    rows, wide, sems, stage, out_sems = refs[total + added + 2 :]
    mark[...] = jnp.zeros_like(mark)
    copies = []
    for i, part, last, value in products(refs[:pieces], weights, columns, rows, wide, sems):
        stage[i, part, :] = value
        if not last:
            continue
        place = out.at[lax.rem(slots[i] + x_ref[0], 4)]
        copies.append(pltpu.make_async_copy(stage.at[i], place, out_sems.at[i]))
        copies[-1].start()
    for copy in copies:
        copy.wait()


def project(columns, shift, pieces, parts_of, slots):
    weights = [part for slot in slots for part in parts_of[slot]]
    counts = tuple(len(parts_of[slot]) for slot in slots)
    count = sum(piece.shape[0] for piece in pieces)
    width = pieces[0].shape[1]
    operands = len(pieces) + len(weights)
    return pl.pallas_call(
        functools.partial(
            project_kernel, pieces=len(pieces), slots=slots, counts=counts, columns=columns
        ),
        in_specs=[SMEM] + [FAR] * operands,
        out_specs=[FAR] * 4,
        out_shape=[jax.ShapeDtypeStruct((count, columns), jnp.bfloat16)] * 4,
        scratch_shapes=scratch_for(count, width, columns, len(slots), operands)
        + [
            pltpu.VMEM((len(slots), count, columns), jnp.bfloat16),
            pltpu.SemaphoreType.DMA((len(slots),)),
        ],
        cost_estimate=LONG,
        compiler_params=LIMIT,
    )(shift, *pieces, *weights)


def project_stack(columns, x, pieces, parts_of, slots, stack=None):
    weights = [part for slot in slots for part in parts_of[slot]]
    counts = tuple(len(parts_of[slot]) for slot in slots)
    count = sum(piece.shape[0] for piece in pieces)
    width = pieces[0].shape[1]
    operands = len(pieces) + len(weights)
    extra = [] if stack is None else [stack]
    return pl.pallas_call(
        functools.partial(
            project_stack_kernel,
            pieces=len(pieces),
            slots=slots,
            counts=counts,
            columns=columns,
            added=len(extra),
        ),
        in_specs=[SMEM] + [FAR] * (operands + len(extra)),
        out_specs=[FAR, VMEM],
        out_shape=[
            jax.ShapeDtypeStruct((4, count, columns), jnp.bfloat16),
            jax.ShapeDtypeStruct((8, HEAD), jnp.float32),
        ],
        input_output_aliases={1 + operands: 0} if extra else {},
        scratch_shapes=scratch_for(count, width, columns, len(slots), operands)
        + [
            pltpu.VMEM((len(slots), count, columns), jnp.bfloat16),
            pltpu.SemaphoreType.DMA((len(slots),)),
        ],
        cost_estimate=BRIEF if len(slots) == 3 else LONG,
        compiler_params=LIMIT,
    )(x, *pieces, *weights, *extra)


def exchange(stack, axis):
    return lax.all_to_all(stack, axis, 0, 0, tiled=True)


def sum_of(stack):
    return jnp.sum(stack.astype(jnp.float32), axis=0).astype(jnp.bfloat16)


def sum_over_y(parts, *earlier):
    received = after([send(part, "y", k) for k, part in enumerate(parts) if k], earlier)
    total = parts[0].astype(jnp.float32)
    for part in received:
        total = total + part.astype(jnp.float32)
    return total.astype(jnp.bfloat16)


def gather_x(block):
    return block, send(block, "x", -1), send(block, "x", -2), send(block, "x", -3)


def attend_kernel(x_ref, z_ref, bound_ref, flag_ref, q_ref, *refs):
    early, late, out = refs[:4], refs[4:8], refs[8]
    kfull, vfull = refs[9:]
    x, z = x_ref[0], z_ref[0]
    c1, c2, c3 = bound_ref[0], bound_ref[1], bound_ref[2]
    for r in range(4):
        lane = lax.rem(x + r, 4)
        for group, offsets in ((early[r], EARLY), (late[r], LATE)):
            for i, offset in enumerate(offsets):
                place = 4 * lax.rem(z + offset, 8) + lane
                at = pl.ds(pl.multiple_of(place * BLOCK, BLOCK), BLOCK)
                kfull[at, :] = group[i * BLOCK : (i + 1) * BLOCK, :HEAD]
                vfull[at, :] = group[i * BLOCK : (i + 1) * BLOCK, HEAD:]

    def first(i):
        return jnp.where(i >= c3, c3, jnp.where(i >= c2, c2, jnp.where(i >= c1, c1, 0)))

    def one_block(index, carry):
        there = 2 * lax.rem(x + lax.div(index, 2), 4) + lax.rem(index, 2)
        base = (4 * there + x) * BLOCK
        mine = pl.ds(pl.multiple_of(index * BLOCK, BLOCK), BLOCK)
        spans = lax.div(base + BLOCK - first(base) + SPAN - 1, SPAN)
        alive = flag_ref[4 * there + x] == 0

        @pl.when(jnp.logical_not(alive))
        def _():
            out[mine, :] = jnp.zeros((BLOCK, HEAD), jnp.bfloat16)

        for n in range(1, LONGEST + 1):

            @pl.when(alive & (spans == n))
            def _():
                keys = n * SPAN
                low = jnp.maximum(base + BLOCK - keys, 0)
                window = pl.ds(pl.multiple_of(low, BLOCK), keys)
                q_at = lax.rem(there - z + 8, 8) * BLOCK
                query = q_ref[pl.ds(pl.multiple_of(q_at, BLOCK), BLOCK), :]
                score = lax.dot_general(
                    query,
                    kfull[window, :],
                    (((1,), (1,)), ((), ())),
                    preferred_element_type=jnp.float32,
                ) * (1.0 / math.sqrt(HEAD))
                row = base + lax.broadcasted_iota(jnp.int32, (BLOCK, 1), 0)
                begin = first(row)
                column = low + lax.broadcasted_iota(jnp.int32, (BLOCK, keys), 1)
                score = jnp.where((column <= row) & (column >= begin), score, -1e30)
                expo = jnp.exp(score - jnp.max(score, axis=-1, keepdims=True))
                norm = jnp.sum(expo, axis=-1, keepdims=True)
                mixed = jnp.dot(
                    expo.astype(jnp.bfloat16), vfull[window, :], preferred_element_type=jnp.float32
                )
                out[mine, :] = (mixed / norm).astype(jnp.bfloat16)

        return carry

    lax.fori_loop(0, 8, one_block, 0)


def attend(x, z, bounds, flags, query, early, late):
    rows = query.shape[0]
    return pl.pallas_call(
        attend_kernel,
        in_specs=[SMEM] * 4 + [VMEM] * 9,
        out_specs=VMEM,
        out_shape=jax.ShapeDtypeStruct((rows, HEAD), jnp.bfloat16),
        scratch_shapes=[pltpu.VMEM((4 * rows, HEAD), jnp.bfloat16)] * 2,
        cost_estimate=BRIEF,
        compiler_params=pltpu.CompilerParams(vmem_limit_bytes=24 * 2**20),
    )(x, z, bounds, flags, query, *early, *late)


def place_kernel(y_ref, *refs):
    parts, outs, whole, sems = refs[:4], refs[4:6], refs[6], refs[7]
    loads = []
    for s in range(4):
        x = lax.rem(y_ref[0] + 4 - s, 4)
        for t in range(2):
            at = pl.ds(pl.multiple_of((4 * t + x) * BLOCK, BLOCK), BLOCK)
            source = parts[s].at[pl.ds(t * BLOCK, BLOCK)]
            loads.append(pltpu.make_async_copy(source, whole.at[at], sems.at[2 + len(loads)]))
    for copy in loads:
        copy.start()
    for copy in loads:
        copy.wait()
    copies = [pltpu.make_async_copy(whole, out, sems.at[i]) for i, out in enumerate(outs)]
    for copy in copies:
        copy.start()
    for copy in copies:
        copy.wait()


def place(y, parts):
    rows = 4 * parts[0].shape[0]
    return pl.pallas_call(
        place_kernel,
        in_specs=[SMEM] + [FAR] * 4,
        out_specs=[FAR] * 2,
        out_shape=[jax.ShapeDtypeStruct((rows, HEAD), jnp.bfloat16)] * 2,
        scratch_shapes=[
            pltpu.VMEM((rows, HEAD), jnp.bfloat16),
            pltpu.SemaphoreType.DMA((10,)),
        ],
        compiler_params=pltpu.CompilerParams(vmem_limit_bytes=58 * 2**20),
    )(y, *parts)


def local(hidden, w_qkv, segment_ids, exit_flags):
    x, y, z = (lax.axis_index(axis).astype(jnp.int32) for axis in ("x", "y", "z"))
    weights = w_qkv[0]
    segment = segment_ids[0]
    steps = jnp.arange(1, 4, dtype=jnp.int32)
    bounds = jnp.sum((segment[None, :] < steps[:, None]).astype(jnp.int32), axis=1)
    x, y, z = (index.reshape(1) for index in (x, y, z))
    shift = lax.rem(x - y + 4, 4)
    blocks = gather_z_ring(hidden[0])
    key_value = jnp.concatenate([weights[:, 1, :], weights[:, 2, :]], axis=1)
    kv_w = gather_x_ring(key_value, (bounds, shift), (blocks[2], blocks[6]))

    def pieces(offsets):
        return [piece for offset in offsets for piece in blocks[offset]]

    near = pieces(EARLY)
    stack, mark = project_stack(256, x, near, kv_w, (0, 1, 3))
    near = after(near, blocks[3], blocks[5])
    own = after(weights[:, 0, :], mark, kv_w[2])
    stack, mark = project_stack(256, x, near, kv_w, (2,), stack)
    q_w = [(part,) for part in gather_x_by_right(own)]
    received = exchange(stack, "y")
    late_parts = project(256, shift, after(pieces(LATE), mark), kv_w, (0, 1, 3, 2))
    early = sum_of(received)
    q_w = after(q_w, late_parts[0], early)
    early = gather_x_by_right(early)
    stack, mark = project_stack(128, x, pieces(range(8)), q_w, (0, 1, 3, 2))
    late = sum_over_y(late_parts, stack)
    query = sum_of(exchange(after(stack, late, early[1], early[3]), "y"))
    mixed = attend(x, z, bounds, exit_flags[0], query, early, gather_x(late))
    quarter = mixed.shape[0] // 4
    moved = [
        lax.ppermute(
            mixed[s * quarter : (s + 1) * quarter],
            ("x", "y"),
            [(4 * i + j, 4 * j + (i + s) % 4) for i in range(4) for j in range(4)],
        )
        for s in range(4)
    ]
    result, given = place(y, moved)
    handed = send(given[None], "phase", 1)
    return (result[None], handed)


def solution(mesh):
    split = Mesh(mesh.devices.reshape(2, 8, 4, 4), ("phase", "z", "x", "y"))
    tok = ("z", "x")
    in_specs = (
        P("phase", tok, "y"),
        P("phase", "y", None, tok),
        P("phase", None),
        P("phase", None),
    )
    out_specs = (P("phase", "y", tok), P("phase", "y", tok))
    return jax.shard_map(local, mesh=split, in_specs=in_specs, out_specs=out_specs, check_vma=False)
```
